32 devices in a mesh: row: 16 (over z, x, core), col: 2 (over y).
Axes of the slice: x: 2, y: 2, z: 4, core: 2. Of those that a mesh axis runs over, the one named last changes fastest.
Arguments:
- inputs: bfloat16 [8192, 5376], P('row', 'col'), may hold values from -6 to 6
- norm_gain: float32 [5376], replicated, may hold values from 0.1 to 1.9
- w_query: bfloat16 [5376, 4096], P('row', 'col'), may hold values from -1 to 1
- w_key: bfloat16 [5376, 2048], P('row', 'col'), may hold values from -2 to 2
- w_value: bfloat16 [5376, 2048], P('row', 'col'), may hold values from -0.078125 to 0.078125
- w_out: bfloat16 [4096, 5376], P('col', 'row'), may hold values from -0.09375 to 0.09375
- q_gain: float32 [128], replicated, may hold values from 0.5 to 5
- k_gain: float32 [128], replicated, may hold values from 0.5 to 5
Outputs:
- attended: bfloat16 [8192, 5376], P('row', 'col')
The draws below stay inside these ranges and needn't reach their ends.
All inputs are finite; a program needn't handle non-finite values.
Results may differ from the reference program's by a relative error of at most 0.017.
Values may be sent and summed in bfloat16 or wider, within the bound.
A program may use at most 128 MiB of HBM per device.

```python
import jax
import jax.numpy as jnp
from jax import lax

D = 5376
HEADS = 32
KVH = 16
HD = 128
WIN = 1024
TOK_DEV = 512
TOKENS = 8192
QW = 4096
KW = 2048
N_ROW = 16
N_COL = 2


def draw_shared(key):
    return jax.random.truncated_normal(jax.random.fold_in(key, 11), -6.0, 6.0, (D, HEADS * HD), jnp.float32)


def draw_w_query(key, part):
    return (draw_shared(key) * D ** (-0.5)).astype(jnp.bfloat16)


def draw_w_key(key, part):
    noise = jax.random.truncated_normal(jax.random.fold_in(key, 12), -6.0, 6.0, (D, KVH * HD), jnp.float32)
    mixed = noise
    return (mixed * D ** (-0.5)).astype(jnp.bfloat16)


def draw_q_gain(key, part):
    inner = jax.random.fold_in(key, 21)
    return jax.random.uniform(inner, (HD,), jnp.float32, 0.6, 1.6)


def draw_k_gain(key, part):
    inner = jax.random.fold_in(key, 22)
    return jax.random.uniform(inner, (HD,), jnp.float32, 0.6, 1.6)


def levels(key, shape, split, low, high):
    loudness = 1.0
    for position, blocks in split:
        heights = jax.random.uniform(jax.random.fold_in(jax.random.fold_in(key, 6), position), (blocks,), jnp.float32, low / len(split), high / len(split))
        loudness = loudness * jnp.repeat(jnp.exp(heights), shape[position] // blocks).reshape((-1,) + (1,) * (len(shape) - 1 - position))
    return loudness


def bell_draw(stream_key, shape, width, reach, pieces=(), kind=jnp.bfloat16):
    array = width * jax.random.normal(stream_key, shape, jnp.float32)
    if pieces:
        array = array * levels(stream_key, shape, pieces, -0.22, 0.18)
    return jnp.clip(array, -reach, reach).astype(kind)


def setup_inputs(seed: int = 0) -> dict:
    key_of = jax.random.split(jax.random.key(seed), 9)
    return {
        "inputs": bell_draw(key_of[0], (TOKENS, D), 1.0, 6.0, ((0, 16), (1, 2))),
        "norm_gain": jnp.clip(1.0 + 0.18 * jax.random.normal(key_of[1], (D,), jnp.float32), 0.1, 1.9),
        "w_query": draw_w_query(jax.random.fold_in(key_of[8], 71), 0),
        "w_key": draw_w_key(jax.random.fold_in(key_of[8], 71), 0),
        "w_value": bell_draw(key_of[4], (D, KW), D ** -0.5, 0.078125, ((0, 16), (1, 2))),
        "w_out": bell_draw(key_of[5], (QW, D), QW ** -0.5, 0.09375, ((0, 2), (1, 16))),
        "q_gain": draw_q_gain(jax.random.fold_in(key_of[8], 71), 0),
        "k_gain": draw_k_gain(jax.random.fold_in(key_of[8], 71), 0),
    }


epsilon = 1e-06
score_scale = 168.0 ** (-0.5)

def rotate_pairs(values, positions):
    half_dim = values.shape[-1] // 2
    frequency = jnp.exp(-(jnp.arange(half_dim, dtype=jnp.float32) * (2.0 / values.shape[-1])) * jnp.log(jnp.float32(10000.0)))
    angles = positions[:, None] * frequency[None, :]
    cosine = jnp.cos(angles)[:, None, :]
    sine = jnp.sin(angles)[:, None, :]
    first = values[..., :half_dim]
    second = values[..., half_dim:]
    return jnp.concatenate([first * cosine - second * sine, second * cosine + first * sine], axis=-1)

def head_rms(values, gain):
    return values * lax.rsqrt(lax.optimization_barrier(jnp.mean(values * values, axis=-1, keepdims=True)) + epsilon) * gain

def reference(inputs, norm_gain, w_query, w_key, w_value, w_out, q_gain, k_gain):
    input_float = inputs.astype(jnp.float32)
    mean_sq = lax.optimization_barrier(jnp.mean(input_float * input_float, axis=1, keepdims=True))
    normed = (input_float * lax.rsqrt(mean_sq + epsilon) * norm_gain).astype(jnp.bfloat16)
    query_proj = jnp.dot(normed, w_query, preferred_element_type=jnp.float32).reshape(TOKENS, HEADS, HD)
    key_proj = jnp.dot(normed, w_key, preferred_element_type=jnp.float32).reshape(TOKENS, KVH, HD)
    value_proj = jnp.dot(normed, w_value, preferred_element_type=jnp.float32).reshape(TOKENS, KVH, HD)
    positions = jnp.arange(TOKENS, dtype=jnp.int32).astype(jnp.float32)
    query_rot = rotate_pairs(head_rms(query_proj, q_gain), positions).astype(jnp.bfloat16)
    key_rot = rotate_pairs(head_rms(key_proj, k_gain), positions).astype(jnp.bfloat16)
    value_rows = value_proj.astype(jnp.bfloat16)
    behind = (WIN - 2) // TOK_DEV + 1
    padding = behind * TOK_DEV
    key_padded = jnp.concatenate([jnp.zeros((padding, KVH, HD), jnp.bfloat16), key_rot], axis=0)
    value_padded = jnp.concatenate([jnp.zeros((padding, KVH, HD), jnp.bfloat16), value_rows], axis=0)

    def attend_block(index):
        start = (index * TOK_DEV).astype(jnp.int32)
        query_block = lax.dynamic_slice_in_dim(query_rot, start, TOK_DEV, 0).reshape(TOK_DEV, KVH, 2, HD)
        key_block = lax.dynamic_slice_in_dim(key_padded, start, padding + TOK_DEV, 0)
        value_block = lax.dynamic_slice_in_dim(value_padded, start, padding + TOK_DEV, 0)
        query_pos = start + jnp.arange(TOK_DEV, dtype=jnp.int32)
        key_pos = start - padding + jnp.arange(padding + TOK_DEV, dtype=jnp.int32)
        scores = jnp.einsum('qhgd,khd->hgqk', query_block.astype(jnp.float32), key_block.astype(jnp.float32)) * score_scale
        allowed = (key_pos[None, :] <= query_pos[:, None]) & (query_pos[:, None] - key_pos[None, :] < WIN) & (key_pos[None, :] >= 0)
        scores = jnp.where(allowed, scores, -1e+30)
        highest = lax.optimization_barrier(jnp.max(scores, axis=-1, keepdims=True))
        weights = jnp.exp(scores - highest)
        probs = (weights / lax.optimization_barrier(jnp.sum(weights, axis=-1, keepdims=True))).astype(jnp.bfloat16)
        heads_out = jnp.einsum('hgqk,khd->qhgd', probs.astype(jnp.float32), value_block.astype(jnp.float32))
        return heads_out.astype(jnp.bfloat16).reshape(TOK_DEV, QW)
    heads_out = lax.map(attend_block, jnp.arange(N_ROW, dtype=jnp.int32)).reshape(TOKENS, QW)
    group_width = QW // N_COL
    summed = jnp.zeros((TOKENS, D), jnp.float32)
    for group in range(N_COL):
        partial_value = jnp.dot(heads_out[:, group * group_width:(group + 1) * group_width], w_out[group * group_width:(group + 1) * group_width], preferred_element_type=jnp.float32)
        summed = summed + partial_value.astype(jnp.bfloat16).astype(jnp.float32)
    return summed.astype(jnp.bfloat16)
```

```python
import jax
import jax.numpy as jnp
from jax import lax
from jax.experimental import pallas as pl
from jax.experimental.pallas import tpu as pltpu
from jax.sharding import PartitionSpec as P

HD = 128
WIN = 1024


epsilon = 1e-06
score_scale = 168.0 ** (-0.5)


def from_behind(block, axis, distance):
    devices = range(lax.axis_size(axis))
    route = [(i - distance, i) for i in devices if i - distance in devices]
    return lax.ppermute(block, axis, route)


def rotation(positions):
    half_dim = HD // 2
    frequency = jnp.exp(
        -(jnp.arange(half_dim, dtype=jnp.float32) * (2.0 / HD)) * jnp.log(jnp.float32(10000.0))
    )
    angles = positions[:, None] * frequency[None, :]
    return jnp.cos(angles), jnp.sin(angles)


def rotate_pairs(values, cosine, sine):
    half_dim = values.shape[-1] // 2
    cosine = cosine[:, None, :]
    sine = sine[:, None, :]
    first = values[..., :half_dim]
    second = values[..., half_dim:]
    return jnp.concatenate(
        [first * cosine - second * sine, second * cosine + first * sine], axis=-1
    )


def head_rms(values, gain):
    return values * lax.rsqrt(jnp.mean(values * values, axis=-1, keepdims=True) + epsilon) * gain


def add_rows(normed, piece):
    return jnp.dot(normed, piece, preferred_element_type=jnp.float32)


def attend(first_ref, q_ref, gain_ref, cos_ref, sin_ref, k_ref, v_ref, out_ref):
    tok_rows, span = q_ref.shape[0], k_ref.shape[0]
    query_at = lax.broadcasted_iota(jnp.int32, (tok_rows, span), 0) + (span - tok_rows)
    key_at = lax.broadcasted_iota(jnp.int32, (tok_rows, span), 1)
    oldest = span - tok_rows - first_ref[0]
    allowed = (key_at <= query_at) & (query_at - key_at < WIN) & (key_at >= oldest)
    for member in range(2):
        columns = slice(member * HD, (member + 1) * HD)
        query = head_rms(q_ref[:, columns], gain_ref[...])
        query = query * cos_ref[...] + pltpu.roll(query, HD // 2, 1) * sin_ref[...]
        scores = (
            lax.dot_general(
                query.astype(jnp.bfloat16),
                k_ref[...],
                (((1,), (1,)), ((), ())),
                preferred_element_type=jnp.float32,
            )
            * score_scale
        )
        scores = jnp.where(allowed, scores, -1e30)
        weights = jnp.exp(scores - jnp.max(scores, axis=-1, keepdims=True))
        probs = (weights / jnp.sum(weights, axis=-1, keepdims=True)).astype(jnp.bfloat16)
        out_ref[:, columns] = jnp.dot(
            probs, v_ref[...], preferred_element_type=jnp.float32
        ).astype(jnp.bfloat16)


def attention(query_proj, q_gain, cosine, sine, key_rows, value_rows, first_pos):
    tok_rows, width = query_proj.shape
    span = key_rows.shape[0]
    whole = lambda i: (0, 0)
    per_head = lambda i: (0, i)
    return pl.pallas_call(
        attend,
        grid=(width // (2 * HD),),
        in_specs=[
            pl.BlockSpec(memory_space=pltpu.SMEM),
            pl.BlockSpec((tok_rows, 2 * HD), per_head),
            pl.BlockSpec((1, HD), whole),
            pl.BlockSpec((tok_rows, HD), whole),
            pl.BlockSpec((tok_rows, HD), whole),
            pl.BlockSpec((span, HD), per_head),
            pl.BlockSpec((span, HD), per_head),
        ],
        out_specs=pl.BlockSpec((tok_rows, 2 * HD), per_head),
        out_shape=jax.ShapeDtypeStruct((tok_rows, width), jnp.bfloat16),
        compiler_params=pltpu.CompilerParams(vmem_limit_bytes=40 * 2**20),
        cost_estimate=pl.CostEstimate(
            flops=4 * tok_rows * span * width,
            bytes_accessed=tok_rows * width * 6 + span * width * 2,
            transcendentals=tok_rows * span * width // HD,
        ),
    )(first_pos.reshape(1), query_proj, q_gain.reshape(1, HD), cosine, sine, key_rows, value_rows)


def swap_col(block):
    return lax.ppermute(block, "col", [(0, 1), (1, 0)])


def gather_channels(inputs):
    if lax.axis_size("col") != 2:
        return lax.all_gather(inputs, "col", axis=1, tiled=True)
    other = swap_col(inputs)
    is_first = lax.axis_index("col") == 0
    return jnp.concatenate(
        [jnp.where(is_first, inputs, other), jnp.where(is_first, other, inputs)], axis=1
    )


def sum_partials(partial_t):
    if lax.axis_size("col") != 2:
        return lax.psum_scatter(partial_t, "col", scatter_dimension=0, tiled=True)
    halves = partial_t.reshape((2, partial_t.shape[0] // 2) + partial_t.shape[1:])
    me = lax.axis_index("col")
    arrived = swap_col(lax.dynamic_index_in_dim(halves, 1 - me, 0, keepdims=False))
    mine = lax.dynamic_index_in_dim(halves, me, 0, keepdims=False)
    return (mine.astype(jnp.float32) + arrived.astype(jnp.float32)).astype(jnp.bfloat16)


def shards(inputs, norm_gain, w_query, w_key, w_value, w_out, q_gain, k_gain):
    tok_rows, local_width = inputs.shape
    kv_local = w_key.shape[1] // HD
    w_kv = lax.all_gather(
        jnp.concatenate([w_key, w_value], axis=1), "row", axis=0, tiled=True
    )
    gathered = gather_channels(inputs)
    w_kv, w_query, gathered = lax.optimization_barrier((w_kv, w_query, gathered))
    input_float = gathered.astype(jnp.float32)
    mean_sq = jnp.mean(input_float * input_float, axis=1, keepdims=True)
    normed = (input_float * lax.rsqrt(mean_sq + epsilon) * norm_gain).astype(jnp.bfloat16)
    normed = lax.optimization_barrier(normed)
    w_query_all = lax.all_gather(w_query, "row", axis=0, tiled=True)
    kv_proj = add_rows(normed, w_kv)
    key_proj = kv_proj[:, : kv_local * HD]
    value_proj = kv_proj[:, kv_local * HD :]
    first_pos = lax.axis_index("row") * tok_rows
    query_pos = first_pos + jnp.arange(tok_rows, dtype=jnp.int32)
    positions = query_pos.astype(jnp.float32)
    cosine, sine = rotation(positions)
    key_rot = rotate_pairs(
        head_rms(key_proj.reshape(tok_rows, kv_local, HD), k_gain), cosine, sine
    ).astype(jnp.bfloat16)
    key_value = jnp.stack(
        [key_rot.reshape(tok_rows, kv_local * HD), value_proj.astype(jnp.bfloat16)]
    )
    behind = (WIN - 2) // tok_rows + 1
    earlier = []
    for offset in range(behind, 0, -1):
        earlier.append(from_behind(key_value, "row", offset))
    window_rows = jnp.concatenate(earlier + [key_value], axis=1)
    w_out_t = w_out.T
    half = w_out_t.shape[0] // 2
    w_query_all, first_half, second_half, window_rows = lax.optimization_barrier(
        (w_query_all, w_out_t[:half], w_out_t[half:], window_rows)
    )
    first_half = lax.all_gather(first_half, "row", axis=0, tiled=True)
    query_proj = add_rows(normed, w_query_all)
    heads_out = attention(
        query_proj,
        q_gain,
        jnp.concatenate([cosine, cosine], axis=1),
        jnp.concatenate([-sine, sine], axis=1),
        window_rows[0],
        window_rows[1],
        first_pos,
    )

    first_half, second_half, heads_out = lax.optimization_barrier(
        (first_half, second_half, heads_out)
    )
    second_half = lax.all_gather(second_half, "row", axis=0, tiled=True)

    def project(columns):
        partial_t = lax.dot_general(
            columns, heads_out, (((1,), (1,)), ((), ())), preferred_element_type=jnp.float32
        ).astype(jnp.bfloat16)
        summed = sum_partials(partial_t)
        return summed.reshape(-1, half, tok_rows)

    both = jnp.concatenate([project(first_half), project(second_half)], axis=1)
    return both.reshape(-1, tok_rows).T


def solution(mesh):
    placed = (
        P("row", "col"),
        P(),
        P("row", "col"),
        P("row", "col"),
        P("row", "col"),
        P("col", "row"),
        P(),
        P(),
    )
    return jax.shard_map(
        shards, mesh=mesh, in_specs=placed, out_specs=P("row", "col"), check_vma=False
    )
```

```python
import jax
import jax.numpy as jnp
from jax import lax
from jax.experimental import pallas as pl
from jax.experimental.pallas import tpu as pltpu
from jax.sharding import PartitionSpec as P

HD = 128
WIN = 1024


epsilon = 1e-06
score_scale = 168.0 ** (-0.5)


def from_behind(block, axis, distance):
    devices = range(lax.axis_size(axis))
    route = [(i - distance, i) for i in devices if i - distance in devices]
    return lax.ppermute(block, axis, route)


def rotation(positions):
    half_dim = HD // 2
    frequency = jnp.exp(
        -(jnp.arange(half_dim, dtype=jnp.float32) * (2.0 / HD)) * jnp.log(jnp.float32(10000.0))
    )
    angles = positions[:, None] * frequency[None, :]
    return jnp.cos(angles), jnp.sin(angles)


def rotate_pairs(values, cosine, sine):
    half_dim = values.shape[-1] // 2
    cosine = cosine[:, None, :]
    sine = sine[:, None, :]
    first = values[..., :half_dim]
    second = values[..., half_dim:]
    return jnp.concatenate(
        [first * cosine - second * sine, second * cosine + first * sine], axis=-1
    )


def head_rms(values, gain):
    return values * lax.rsqrt(jnp.mean(values * values, axis=-1, keepdims=True) + epsilon) * gain


def add_rows(normed, piece):
    return jnp.dot(normed, piece, preferred_element_type=jnp.float32)


def attend(first_ref, q_ref, gain_ref, cos_ref, sin_ref, k_ref, v_ref, out_ref):
    tok_rows, span = q_ref.shape[0], k_ref.shape[0]
    query_at = lax.broadcasted_iota(jnp.int32, (tok_rows, span), 0) + (span - tok_rows)
    key_at = lax.broadcasted_iota(jnp.int32, (tok_rows, span), 1)
    oldest = span - tok_rows - first_ref[0]
    allowed = (key_at <= query_at) & (query_at - key_at < WIN) & (key_at >= oldest)
    for member in range(2):
        columns = slice(member * HD, (member + 1) * HD)
        query = head_rms(q_ref[:, columns], gain_ref[...])
        query = query * cos_ref[...] + pltpu.roll(query, HD // 2, 1) * sin_ref[...]
        scores = (
            lax.dot_general(
                query.astype(jnp.bfloat16),
                k_ref[...],
                (((1,), (1,)), ((), ())),
                preferred_element_type=jnp.float32,
            )
            * score_scale
        )
        scores = jnp.where(allowed, scores, -1e30)
        weights = jnp.exp(scores - jnp.max(scores, axis=-1, keepdims=True))
        probs = (weights / jnp.sum(weights, axis=-1, keepdims=True)).astype(jnp.bfloat16)
        out_ref[:, columns] = jnp.dot(
            probs, v_ref[...], preferred_element_type=jnp.float32
        ).astype(jnp.bfloat16)


def attention(query_proj, q_gain, cosine, sine, key_rows, value_rows, first_pos):
    tok_rows, width = query_proj.shape
    span = key_rows.shape[0]
    whole = lambda i: (0, 0)
    per_head = lambda i: (0, i)
    return pl.pallas_call(
        attend,
        grid=(width // (2 * HD),),
        in_specs=[
            pl.BlockSpec(memory_space=pltpu.SMEM),
            pl.BlockSpec((tok_rows, 2 * HD), per_head),
            pl.BlockSpec((1, HD), whole),
            pl.BlockSpec((tok_rows, HD), whole),
            pl.BlockSpec((tok_rows, HD), whole),
            pl.BlockSpec((span, HD), per_head),
            pl.BlockSpec((span, HD), per_head),
        ],
        out_specs=pl.BlockSpec((tok_rows, 2 * HD), per_head),
        out_shape=jax.ShapeDtypeStruct((tok_rows, width), jnp.bfloat16),
        compiler_params=pltpu.CompilerParams(vmem_limit_bytes=40 * 2**20),
        cost_estimate=pl.CostEstimate(
            flops=4 * tok_rows * span * width,
            bytes_accessed=tok_rows * width * 6 + span * width * 2,
            transcendentals=tok_rows * span * width // HD,
        ),
    )(first_pos.reshape(1), query_proj, q_gain.reshape(1, HD), cosine, sine, key_rows, value_rows)


def swap_col(block):
    return lax.ppermute(block, "col", [(0, 1), (1, 0)])


def gather_channels(inputs):
    if lax.axis_size("col") != 2:
        return lax.all_gather(inputs, "col", axis=1, tiled=True)
    other = swap_col(inputs)
    is_first = lax.axis_index("col") == 0
    return jnp.concatenate(
        [jnp.where(is_first, inputs, other), jnp.where(is_first, other, inputs)], axis=1
    )


def project(heads_out, w_out_t):
    def partial_sums(columns):
        return lax.dot_general(
            columns, heads_out, (((1,), (1,)), ((), ())), preferred_element_type=jnp.float32
        ).astype(jnp.bfloat16)

    if lax.axis_size("col") != 2:
        return lax.psum_scatter(partial_sums(w_out_t), "col", scatter_dimension=0, tiled=True)
    half = w_out_t.shape[0] // 2
    me = lax.axis_index("col")
    sent = partial_sums(lax.dynamic_slice_in_dim(w_out_t, (1 - me) * half, half, 0))
    arrived = swap_col(sent)
    mine = partial_sums(lax.dynamic_slice_in_dim(w_out_t, me * half, half, 0))
    return (mine.astype(jnp.float32) + arrived.astype(jnp.float32)).astype(jnp.bfloat16)


def window_blocks(block):
    n_row = lax.axis_size("row")
    behind = (WIN - 2) // block.shape[1] + 1
    if behind != 2 or n_row % 2:
        return [from_behind(block, "row", offset) for offset in range(behind, 0, -1)] + [block]
    second = from_behind(block, "row", 2)
    odd = lax.axis_index("row") % 2 == 1
    first = lax.ppermute(
        jnp.where(odd, second, block), "row", [(i, i ^ 1) for i in range(n_row)]
    )
    return [second, first, block]


def shards(inputs, norm_gain, w_query, w_key, w_value, w_out, q_gain, k_gain):
    tok_rows, local_width = inputs.shape
    kv_local = w_key.shape[1] // HD
    w_qkv = lax.all_gather(
        jnp.concatenate([w_key, w_value, w_query], axis=1), "row", axis=0, tiled=True
    )
    gathered = gather_channels(inputs)
    w_qkv, w_out_t, gathered = lax.optimization_barrier((w_qkv, w_out.T, gathered))
    w_out_t = lax.all_gather(w_out_t, "row", axis=0, tiled=True)
    input_float = gathered.astype(jnp.float32)
    mean_sq = jnp.mean(input_float * input_float, axis=1, keepdims=True)
    normed = (input_float * lax.rsqrt(mean_sq + epsilon) * norm_gain).astype(jnp.bfloat16)
    normed = lax.optimization_barrier(normed)
    kv_proj = add_rows(normed, w_qkv[:, : 2 * kv_local * HD])
    query_proj = add_rows(normed, w_qkv[:, 2 * kv_local * HD :])
    key_proj = kv_proj[:, : kv_local * HD]
    value_proj = kv_proj[:, kv_local * HD :]
    first_pos = lax.axis_index("row") * tok_rows
    query_pos = first_pos + jnp.arange(tok_rows, dtype=jnp.int32)
    positions = query_pos.astype(jnp.float32)
    cosine, sine = rotation(positions)
    key_rot = rotate_pairs(
        head_rms(key_proj.reshape(tok_rows, kv_local, HD), k_gain), cosine, sine
    ).astype(jnp.bfloat16)
    key_value = jnp.stack(
        [key_rot.reshape(tok_rows, kv_local * HD), value_proj.astype(jnp.bfloat16)]
    )
    window_rows = jnp.concatenate(window_blocks(key_value), axis=1)
    heads_out = attention(
        query_proj,
        q_gain,
        jnp.concatenate([cosine, cosine], axis=1),
        jnp.concatenate([-sine, sine], axis=1),
        window_rows[0],
        window_rows[1],
        first_pos,
    )

    return project(heads_out, w_out_t).T


def solution(mesh):
    placed = (
        P("row", "col"),
        P(),
        P("row", "col"),
        P("row", "col"),
        P("row", "col"),
        P("col", "row"),
        P(),
        P(),
    )
    return jax.shard_map(
        shards, mesh=mesh, in_specs=placed, out_specs=P("row", "col"), check_vma=False
    )
```

```python
import jax
import jax.numpy as jnp
from jax import lax
from jax.experimental import pallas as pl
from jax.experimental.pallas import tpu as pltpu
from jax.sharding import PartitionSpec as P

HD = 128
WIN = 1024


epsilon = 1e-06
score_scale = 168.0 ** (-0.5)


def from_behind(block, axis, distance):
    devices = range(lax.axis_size(axis))
    route = [(i - distance, i) for i in devices if i - distance in devices]
    return lax.ppermute(block, axis, route)


def rotation(positions):
    half_dim = HD // 2
    frequency = jnp.exp(
        -(jnp.arange(half_dim, dtype=jnp.float32) * (2.0 / HD)) * jnp.log(jnp.float32(10000.0))
    )
    angles = positions[:, None] * frequency[None, :]
    return jnp.cos(angles), jnp.sin(angles)


def rotate_pairs(values, cosine, sine):
    half_dim = values.shape[-1] // 2
    cosine = cosine[:, None, :]
    sine = sine[:, None, :]
    first = values[..., :half_dim]
    second = values[..., half_dim:]
    return jnp.concatenate(
        [first * cosine - second * sine, second * cosine + first * sine], axis=-1
    )


def head_rms(values, gain):
    return values * lax.rsqrt(jnp.mean(values * values, axis=-1, keepdims=True) + epsilon) * gain


def add_rows(normed, piece):
    return jnp.dot(normed, piece, preferred_element_type=jnp.float32)


def attend(first_ref, q_ref, gain_ref, cos_ref, sin_ref, k_ref, v_ref, out_ref):
    tok_rows, span = q_ref.shape[0], k_ref.shape[0]
    query_at = lax.broadcasted_iota(jnp.int32, (tok_rows, span), 0) + (span - tok_rows)
    key_at = lax.broadcasted_iota(jnp.int32, (tok_rows, span), 1)
    oldest = span - tok_rows - first_ref[0]
    allowed = (key_at <= query_at) & (query_at - key_at < WIN) & (key_at >= oldest)
    for member in range(2):
        columns = slice(member * HD, (member + 1) * HD)
        query = head_rms(q_ref[:, columns], gain_ref[...])
        query = query * cos_ref[...] + pltpu.roll(query, HD // 2, 1) * sin_ref[...]
        scores = (
            lax.dot_general(
                query.astype(jnp.bfloat16),
                k_ref[...],
                (((1,), (1,)), ((), ())),
                preferred_element_type=jnp.float32,
            )
            * score_scale
        )
        scores = jnp.where(allowed, scores, -1e30)
        weights = jnp.exp(scores - jnp.max(scores, axis=-1, keepdims=True))
        probs = (weights / jnp.sum(weights, axis=-1, keepdims=True)).astype(jnp.bfloat16)
        out_ref[:, columns] = jnp.dot(
            probs, v_ref[...], preferred_element_type=jnp.float32
        ).astype(jnp.bfloat16)


def attention(query_proj, q_gain, cosine, sine, key_rows, value_rows, first_pos):
    tok_rows, width = query_proj.shape
    span = key_rows.shape[0]
    whole = lambda i: (0, 0)
    per_head = lambda i: (0, i)
    return pl.pallas_call(
        attend,
        grid=(width // (2 * HD),),
        in_specs=[
            pl.BlockSpec(memory_space=pltpu.SMEM),
            pl.BlockSpec((tok_rows, 2 * HD), per_head),
            pl.BlockSpec((1, HD), whole),
            pl.BlockSpec((tok_rows, HD), whole),
            pl.BlockSpec((tok_rows, HD), whole),
            pl.BlockSpec((span, HD), per_head),
            pl.BlockSpec((span, HD), per_head),
        ],
        out_specs=pl.BlockSpec((tok_rows, 2 * HD), per_head),
        out_shape=jax.ShapeDtypeStruct((tok_rows, width), jnp.bfloat16),
        compiler_params=pltpu.CompilerParams(vmem_limit_bytes=40 * 2**20),
        cost_estimate=pl.CostEstimate(
            flops=4 * tok_rows * span * width,
            bytes_accessed=tok_rows * width * 6 + span * width * 2,
            transcendentals=tok_rows * span * width // HD,
        ),
    )(first_pos.reshape(1), query_proj, q_gain.reshape(1, HD), cosine, sine, key_rows, value_rows)


def swap_col(block):
    return lax.ppermute(block, "col", [(0, 1), (1, 0)])


def gather_channels(inputs):
    if lax.axis_size("col") != 2:
        return lax.all_gather(inputs, "col", axis=1, tiled=True)
    other = swap_col(inputs)
    is_first = lax.axis_index("col") == 0
    return jnp.concatenate(
        [jnp.where(is_first, inputs, other), jnp.where(is_first, other, inputs)], axis=1
    )


def whole_rows(w_out_t):
    n_row = lax.axis_size("row")
    half = n_row // 2
    route = [(2 * i + 1, 2 * (i + half)) for i in range(half)]
    route += [(2 * (i + half), 2 * i + 1) for i in range(half)]
    moved = lax.ppermute(w_out_t, ("row", "col"), route)
    keeps = (lax.axis_index("row") // half) == lax.axis_index("col")
    return jnp.where(keeps, w_out_t, moved)


def partial_sums(columns, heads_out):
    return lax.dot_general(
        columns, heads_out, (((1,), (1,)), ((), ())), preferred_element_type=jnp.float32
    ).astype(jnp.bfloat16)


def project(heads_out, w_out_t, paired):
    if not paired:
        partial_t = partial_sums(w_out_t, heads_out)
        return lax.psum_scatter(partial_t, "col", scatter_dimension=0, tiled=True)
    other = swap_col(heads_out)
    heads_out, other, w_out_t = lax.optimization_barrier((heads_out, other, w_out_t))
    is_first = lax.axis_index("col") == 0
    half = w_out_t.shape[0] // 2
    total = partial_sums(w_out_t[:half], jnp.where(is_first, heads_out, other)).astype(jnp.float32)
    total = total + partial_sums(w_out_t[half:], jnp.where(is_first, other, heads_out))
    return total.astype(jnp.bfloat16)


def window_blocks(block):
    n_row = lax.axis_size("row")
    behind = (WIN - 2) // block.shape[1] + 1
    if behind != 2 or n_row % 2:
        return [from_behind(block, "row", offset) for offset in range(behind, 0, -1)] + [block]
    second = from_behind(block, "row", 2)
    odd = lax.axis_index("row") % 2 == 1
    first = lax.ppermute(
        jnp.where(odd, second, block), "row", [(i, i ^ 1) for i in range(n_row)]
    )
    return [second, first, block]


def shards(inputs, norm_gain, w_query, w_key, w_value, w_out, q_gain, k_gain):
    tok_rows, local_width = inputs.shape
    kv_local = w_key.shape[1] // HD
    paired = lax.axis_size("col") == 2 and lax.axis_size("row") % 2 == 0
    w_kv = lax.all_gather(
        jnp.concatenate([w_key, w_value], axis=1), "row", axis=0, tiled=True
    )
    gathered = gather_channels(inputs)
    w_out_t = whole_rows(w_out.T) if paired else w_out.T
    w_kv, w_query, w_out_t, gathered = lax.optimization_barrier(
        (w_kv, w_query, w_out_t, gathered)
    )
    w_query_all = lax.all_gather(w_query, "row", axis=0, tiled=True)
    input_float = gathered.astype(jnp.float32)
    mean_sq = jnp.mean(input_float * input_float, axis=1, keepdims=True)
    normed = (input_float * lax.rsqrt(mean_sq + epsilon) * norm_gain).astype(jnp.bfloat16)
    normed = lax.optimization_barrier(normed)
    kv_proj = add_rows(normed, w_kv)
    key_proj = kv_proj[:, : kv_local * HD]
    value_proj = kv_proj[:, kv_local * HD :]
    first_pos = lax.axis_index("row") * tok_rows
    query_pos = first_pos + jnp.arange(tok_rows, dtype=jnp.int32)
    positions = query_pos.astype(jnp.float32)
    cosine, sine = rotation(positions)
    key_rot = rotate_pairs(
        head_rms(key_proj.reshape(tok_rows, kv_local, HD), k_gain), cosine, sine
    ).astype(jnp.bfloat16)
    key_value = jnp.stack(
        [key_rot.reshape(tok_rows, kv_local * HD), value_proj.astype(jnp.bfloat16)]
    )
    window_rows = jnp.concatenate(window_blocks(key_value), axis=1)
    w_query_all, w_out_t, window_rows = lax.optimization_barrier(
        (w_query_all, w_out_t, window_rows)
    )
    w_out_t = lax.all_gather(w_out_t, "row", axis=0, tiled=True)
    query_proj = add_rows(normed, w_query_all)
    heads_out = attention(
        query_proj,
        q_gain,
        jnp.concatenate([cosine, cosine], axis=1),
        jnp.concatenate([-sine, sine], axis=1),
        window_rows[0],
        window_rows[1],
        first_pos,
    )

    return project(heads_out, w_out_t, paired).T


def solution(mesh):
    placed = (
        P("row", "col"),
        P(),
        P("row", "col"),
        P("row", "col"),
        P("row", "col"),
        P("col", "row"),
        P(),
        P(),
    )
    return jax.shard_map(
        shards, mesh=mesh, in_specs=placed, out_specs=P("row", "col"), check_vma=False
    )
```

```python
import jax
import jax.numpy as jnp
from jax import lax
from jax.experimental import pallas as pl
from jax.experimental.pallas import tpu as pltpu
from jax.sharding import PartitionSpec as P

HD = 128
WIN = 1024


epsilon = 1e-06
score_scale = 168.0 ** (-0.5)


def from_behind(block, axis, distance):
    devices = range(lax.axis_size(axis))
    route = [(i - distance, i) for i in devices if i - distance in devices]
    return lax.ppermute(block, axis, route)


def rotation(positions):
    half_dim = HD // 2
    frequency = jnp.exp(
        -(jnp.arange(half_dim, dtype=jnp.float32) * (2.0 / HD)) * jnp.log(jnp.float32(10000.0))
    )
    angles = positions[:, None] * frequency[None, :]
    return jnp.cos(angles), jnp.sin(angles)


def rotate_pairs(values, cosine, sine):
    half_dim = values.shape[-1] // 2
    cosine = cosine[:, None, :]
    sine = sine[:, None, :]
    first = values[..., :half_dim]
    second = values[..., half_dim:]
    return jnp.concatenate(
        [first * cosine - second * sine, second * cosine + first * sine], axis=-1
    )


def head_rms(values, gain):
    return values * lax.rsqrt(jnp.mean(values * values, axis=-1, keepdims=True) + epsilon) * gain


def add_rows(normed, piece):
    return jnp.dot(normed, piece, preferred_element_type=jnp.float32)


def attend(first_ref, q_ref, gain_ref, cos_ref, sin_ref, k_ref, v_ref, out_ref):
    tok_rows, span = q_ref.shape[0], k_ref.shape[0]
    query_at = lax.broadcasted_iota(jnp.int32, (tok_rows, span), 0) + (span - tok_rows)
    key_at = lax.broadcasted_iota(jnp.int32, (tok_rows, span), 1)
    oldest = span - tok_rows - first_ref[0]
    allowed = (key_at <= query_at) & (query_at - key_at < WIN) & (key_at >= oldest)
    for member in range(2):
        columns = slice(member * HD, (member + 1) * HD)
        query = head_rms(q_ref[:, columns], gain_ref[...])
        query = query * cos_ref[...] + pltpu.roll(query, HD // 2, 1) * sin_ref[...]
        scores = (
            lax.dot_general(
                query.astype(jnp.bfloat16),
                k_ref[...],
                (((1,), (1,)), ((), ())),
                preferred_element_type=jnp.float32,
            )
            * score_scale
        )
        scores = jnp.where(allowed, scores, -1e30)
        weights = jnp.exp(scores - jnp.max(scores, axis=-1, keepdims=True))
        probs = (weights / jnp.sum(weights, axis=-1, keepdims=True)).astype(jnp.bfloat16)
        out_ref[:, columns] = jnp.dot(
            probs, v_ref[...], preferred_element_type=jnp.float32
        ).astype(jnp.bfloat16)


def attention(query_proj, q_gain, cosine, sine, key_rows, value_rows, first_pos):
    tok_rows, width = query_proj.shape
    span = key_rows.shape[0]
    whole = lambda i: (0, 0)
    per_head = lambda i: (0, i)
    return pl.pallas_call(
        attend,
        grid=(width // (2 * HD),),
        in_specs=[
            pl.BlockSpec(memory_space=pltpu.SMEM),
            pl.BlockSpec((tok_rows, 2 * HD), per_head),
            pl.BlockSpec((1, HD), whole),
            pl.BlockSpec((tok_rows, HD), whole),
            pl.BlockSpec((tok_rows, HD), whole),
            pl.BlockSpec((span, HD), per_head),
            pl.BlockSpec((span, HD), per_head),
        ],
        out_specs=pl.BlockSpec((tok_rows, 2 * HD), per_head),
        out_shape=jax.ShapeDtypeStruct((tok_rows, width), jnp.bfloat16),
        compiler_params=pltpu.CompilerParams(vmem_limit_bytes=40 * 2**20),
        cost_estimate=pl.CostEstimate(
            flops=4 * tok_rows * span * width,
            bytes_accessed=tok_rows * width * 6 + span * width * 2,
            transcendentals=tok_rows * span * width // HD,
        ),
    )(first_pos.reshape(1), query_proj, q_gain.reshape(1, HD), cosine, sine, key_rows, value_rows)


def swap_col(block):
    return lax.ppermute(block, "col", [(0, 1), (1, 0)])


def gather_channels(inputs):
    if lax.axis_size("col") != 2:
        return lax.all_gather(inputs, "col", axis=1, tiled=True)
    other = swap_col(inputs)
    is_first = lax.axis_index("col") == 0
    return jnp.concatenate(
        [jnp.where(is_first, inputs, other), jnp.where(is_first, other, inputs)], axis=1
    )


def whole_rows(w_out_t):
    n_row = lax.axis_size("row")
    half = n_row // 2
    route = [(2 * i + 1, 2 * (i + half)) for i in range(half)]
    route += [(2 * (i + half), 2 * i + 1) for i in range(half)]
    moved = lax.ppermute(w_out_t, ("row", "col"), route)
    keeps = (lax.axis_index("row") // half) == lax.axis_index("col")
    return jnp.where(keeps, w_out_t, moved)


def partial_sums(columns, heads_out):
    return lax.dot_general(
        columns, heads_out, (((1,), (1,)), ((), ())), preferred_element_type=jnp.float32
    ).astype(jnp.bfloat16)


def project(heads_out, w_out_t, paired):
    if not paired:
        partial_t = partial_sums(w_out_t, heads_out)
        return lax.psum_scatter(partial_t, "col", scatter_dimension=0, tiled=True)
    other = swap_col(heads_out)
    is_first = lax.axis_index("col") == 0
    both = jnp.stack([jnp.where(is_first, heads_out, other), jnp.where(is_first, other, heads_out)])
    both, w_out_t = lax.optimization_barrier((both, w_out_t))
    groups = w_out_t.reshape(2, w_out_t.shape[0] // 2, w_out_t.shape[1])
    return lax.dot_general(
        groups, both, (((0, 2), (0, 2)), ((), ())), preferred_element_type=jnp.float32
    ).astype(jnp.bfloat16)


def window_blocks(block):
    n_row = lax.axis_size("row")
    behind = (WIN - 2) // block.shape[1] + 1
    if behind != 2 or n_row % 2:
        return [from_behind(block, "row", offset) for offset in range(behind, 0, -1)] + [block]
    second = from_behind(block, "row", 2)
    odd = lax.axis_index("row") % 2 == 1
    first = lax.ppermute(
        jnp.where(odd, second, block), "row", [(i, i ^ 1) for i in range(n_row)]
    )
    return [second, first, block]


def shards(inputs, norm_gain, w_query, w_key, w_value, w_out, q_gain, k_gain):
    tok_rows, local_width = inputs.shape
    kv_local = w_key.shape[1] // HD
    paired = lax.axis_size("col") == 2 and lax.axis_size("row") % 2 == 0
    w_kv = lax.all_gather(
        jnp.concatenate([w_key, w_value], axis=1), "row", axis=0, tiled=True
    )
    gathered = gather_channels(inputs)
    w_out_t = whole_rows(w_out.T) if paired else w_out.T
    w_kv, w_query, w_out_t, gathered = lax.optimization_barrier(
        (w_kv, w_query, w_out_t, gathered)
    )
    w_query_all = lax.all_gather(w_query, "row", axis=0, tiled=True)
    input_float = gathered.astype(jnp.float32)
    mean_sq = jnp.mean(input_float * input_float, axis=1, keepdims=True)
    normed = (input_float * lax.rsqrt(mean_sq + epsilon) * norm_gain).astype(jnp.bfloat16)
    normed = lax.optimization_barrier(normed)
    kv_proj = add_rows(normed, w_kv)
    key_proj = kv_proj[:, : kv_local * HD]
    value_proj = kv_proj[:, kv_local * HD :]
    first_pos = lax.axis_index("row") * tok_rows
    query_pos = first_pos + jnp.arange(tok_rows, dtype=jnp.int32)
    positions = query_pos.astype(jnp.float32)
    cosine, sine = rotation(positions)
    key_rot = rotate_pairs(
        head_rms(key_proj.reshape(tok_rows, kv_local, HD), k_gain), cosine, sine
    ).astype(jnp.bfloat16)
    key_value = jnp.stack(
        [key_rot.reshape(tok_rows, kv_local * HD), value_proj.astype(jnp.bfloat16)]
    )
    window_rows = jnp.concatenate(window_blocks(key_value), axis=1)
    w_query_all, w_out_t, window_rows = lax.optimization_barrier(
        (w_query_all, w_out_t, window_rows)
    )
    w_out_t = lax.all_gather(w_out_t, "row", axis=0, tiled=True)
    query_proj = add_rows(normed, w_query_all)
    heads_out = attention(
        query_proj,
        q_gain,
        jnp.concatenate([cosine, cosine], axis=1),
        jnp.concatenate([-sine, sine], axis=1),
        window_rows[0],
        window_rows[1],
        first_pos,
    )

    return project(heads_out, w_out_t, paired).T


def solution(mesh):
    placed = (
        P("row", "col"),
        P(),
        P("row", "col"),
        P("row", "col"),
        P("row", "col"),
        P("col", "row"),
        P(),
        P(),
    )
    return jax.shard_map(
        shards, mesh=mesh, in_specs=placed, out_specs=P("row", "col"), check_vma=False
    )
```
